32 devices in a mesh: fsdp: 4 (over x, core), seq: 8 (over z, y).
Axes of the slice: x: 2, y: 2, z: 4, core: 2. Of those that a mesh axis runs over, the one named last changes fastest.
Arguments:
- qkv: bfloat16 [4, 1024, 6144], P('fsdp', 'seq'), may hold values from -128 to 128
- resid: bfloat16 [4, 1024, 2048], P('fsdp', 'seq'), may hold values from -0.625 to 0.625
- earlier: float32 [4, 1024, 2048], P('fsdp', 'seq'), may hold values from -12 to 12
- lengths: int32 [4, 12], P('fsdp'), may hold values from 1 to 128, 1024 in all within a row
- teacher_out: bfloat16 [2048, 2048], P('seq', 'fsdp'), may hold values from -6 to 6
- student_out: bfloat16 [2048, 2048], P('seq', 'fsdp'), may hold values from -6 to 6
Outputs:
- targets: float32 [4, 1024, 2048], P('fsdp', 'seq')
- teacher_new: bfloat16 [2048, 2048], P('seq', 'fsdp')
The draws below stay inside these ranges and needn't reach their ends.
Inputs may be any that keep to these rules, and one draw needn't show every extreme that they name: Each pack's 12 utterance lengths add up to its 1024 frames, and one of them is exactly 128.
All inputs are finite; a program needn't handle non-finite values.
Results may differ from the reference program's by a relative error of at most 0.0019.
Values may be sent and summed in bfloat16 or wider, within the bound.
A program may use at most 64 MiB of HBM per device.

```python
import math
import jax
import jax.numpy as jnp
import numpy as np
from jax import lax

D = 2048
HEADS = 32
HEAD_DIM = 64
TOP_K = 8
UTTS = 12
FRAMES = 1024
UTT_MAX = 128
PACKS = 4


def draw_qkv(key, part):
    keys_list = jax.random.split(key, 1)
    shape_full = (PACKS, FRAMES, 3, HEADS, HEAD_DIM)
    values_base = jax.random.normal(keys_list[0], shape_full, jnp.float32)
    return values_base.reshape(PACKS, FRAMES, 3 * D).astype(jnp.bfloat16)


def level_of(rng, extent, cuts, low, top_value):
    def one(dim, parts):
        steps = jax.random.uniform(jax.random.fold_in(jax.random.fold_in(rng, 6), dim), (parts,), jnp.float32, low / len(cuts), top_value / len(cuts))
        return jnp.repeat(jnp.exp(steps), extent[dim] // parts).reshape((-1,) + (1,) * (len(extent) - dim - 1))

    gain = one(*cuts[0])
    for cut in cuts[1:]:
        gain = gain * one(*cut)
    return gain


def profile(number_of, total, limit, skew):
    weights = [(1 << 20) // math.isqrt(rank ** skew) + 1 for rank in range(2, number_of + 1)]
    spare, given = total - limit - (number_of - 1), [1] * (number_of - 1)
    while spare > 0:
        free = [i for i in range(number_of - 1) if given[i] < limit]
        pool, budget = sum([weights[i] for i in free]), spare
        for i in free:
            more = min(limit - given[i], max(1, budget * weights[i] // pool), spare)
            given[i] = given[i] + more
            spare = spare - more
    return np.array([limit] + given)


def ragged(key, count, total, most, slope):
    if count == 2:
        one = jax.random.randint(key, (), max(1, total - most), min(most, total - 1) + 1)
        return jnp.stack([one, total - one])
    tallies = jnp.asarray(profile(count, total, most, slope), jnp.int32)
    twos = (count - 1) // 2
    donor, receiver = tallies[1:1 + 2 * twos:2], tallies[2:2 + 2 * twos:2]
    margin = jnp.minimum(donor - 1, most - receiver)
    moved = jax.random.randint(jax.random.fold_in(key, 1), (twos,), 0, 1 << 20) % (margin + 1)
    tallies = tallies.at[1:1 + 2 * twos:2].set(donor - moved).at[2:2 + 2 * twos:2].set(receiver + moved)
    return tallies[jax.random.permutation(jax.random.fold_in(key, 2), count)]


def gaussian(own_key, shape, deviation, bound, cuts=(), held_as=jnp.bfloat16):
    array = deviation * jax.random.normal(own_key, shape, jnp.float32)
    if cuts:
        array = array * level_of(own_key, shape, cuts, -0.22, 0.18)
    return jnp.clip(array, -bound, bound).astype(held_as)


def setup_inputs(seed: int = 0) -> dict:
    arg_keys = jax.random.split(jax.random.key(seed), 7)
    qkv = draw_qkv(jax.random.fold_in(arg_keys[6], 71), 0)
    resid = gaussian(arg_keys[1], (PACKS, FRAMES, D), 0.1, 0.625, ((0, 4), (1, 8)))
    earlier = gaussian(arg_keys[2], (PACKS, FRAMES, D), 2.0, 12.0, ((0, 4), (1, 8)), jnp.float32)
    lengths = jax.vmap(lambda own: ragged(own, UTTS, FRAMES, UTT_MAX, 1))(jax.random.split(arg_keys[3], PACKS)).reshape((PACKS, UTTS)).astype(jnp.int32)
    teacher_out = gaussian(arg_keys[4], (D, D), 1.0, 6.0, ((0, 8), (1, 4)))
    student_out = gaussian(arg_keys[5], (D, D), 1.0, 6.0, ((0, 8), (1, 4)))
    return dict(qkv=qkv, resid=resid, earlier=earlier, lengths=lengths, teacher_out=teacher_out, student_out=student_out)


ema_decay = 0.9
norm_epsilon = 1e-05
masked_score = -1e+30

def segment_ids(utt_lengths, frames):
    utt_ends = jnp.cumsum(utt_lengths).astype(jnp.int32)
    places = jnp.arange(frames, dtype=jnp.int32)
    return lax.optimization_barrier(jnp.sum((places[:, None] >= utt_ends[None, :]).astype(jnp.int32), axis=1))

def attend_dense(stacked, segment):
    inverse_root = 1.0 / math.sqrt(stacked.shape[-1])
    moved = jnp.transpose(stacked.astype(jnp.float32), (2, 1, 0, 3))
    allowed = segment[:, None] == segment[None, :]

    def one_head(head_rows):
        scores = jnp.dot(head_rows[0], head_rows[1].T, precision=lax.Precision.HIGHEST) * inverse_root
        scores = jnp.where(allowed, scores, masked_score)
        row_max = lax.optimization_barrier(jnp.max(scores, axis=1, keepdims=True))
        weights = jnp.exp(scores - row_max)
        row_total = lax.optimization_barrier(jnp.sum(weights, axis=1, keepdims=True))
        rounded = lax.optimization_barrier(weights.astype(jnp.bfloat16)).astype(jnp.float32)
        summed = jnp.dot(rounded, head_rows[2], precision=lax.Precision.HIGHEST)
        return (summed / row_total).astype(jnp.bfloat16)
    outputs = lax.map(one_head, moved)
    return jnp.transpose(outputs, (1, 0, 2)).reshape(stacked.shape[0], -1)

def reference(qkv, resid, earlier, lengths, teacher_out, student_out):
    teacher_new = (ema_decay * teacher_out.astype(jnp.float32) + (1.0 - ema_decay) * student_out.astype(jnp.float32)).astype(jnp.bfloat16)

    def one_pack(pack_args):
        pack_qkv, pack_resid, pack_earlier, pack_lengths = pack_args
        segment = segment_ids(pack_lengths, FRAMES)
        stacked = pack_qkv.reshape(FRAMES, 3, HEADS, HEAD_DIM)
        mixed = attend_dense(stacked, segment)
        branch = jnp.dot(mixed, teacher_new, preferred_element_type=jnp.float32) / math.sqrt(D)
        summed = pack_resid.astype(jnp.float32) + branch
        centered = summed - lax.optimization_barrier(jnp.mean(summed, axis=1, keepdims=True))
        normed = centered * lax.rsqrt(lax.optimization_barrier(jnp.mean(centered * centered, axis=1, keepdims=True)) + norm_epsilon)
        return (pack_earlier + normed) / TOP_K
    targets = lax.map(one_pack, (qkv, resid, earlier, lengths))
    return (targets, teacher_new)
```

```python
import functools
import math

import jax
import jax.numpy as jnp
from jax import lax
from jax.experimental import pallas as pl
from jax.experimental.pallas import tpu as pltpu
from jax.sharding import PartitionSpec as P

HEADS = 32
HEAD_DIM = 64
TOP_K = 8
PAIR = 2

ema_decay = 0.9
norm_epsilon = 1e-05
masked_score = -1e30
log2_e = math.log2(math.e)


def body(
    F, S, H,
    len_ref, qkv_ref, resid_ref, earlier_ref, tea_ref, stu_ref,
    out_ref, new_ref,
    q_buf, kv_buf, mixed, wbuf, bias, psend, precv, acc,
    yx_s, yx_r, loc, ha_s, ha_r, wz_s, wz_r, wx_s, wx_r, wc_s, wc_r, pa_s, pa_r,
):
    T = qkv_ref.shape[0]
    Dm = resid_ref.shape[1]
    cw = Dm // S
    hd = Dm // HEADS
    hp = cw // hd
    R = S // PAIR
    G = F // PAIR
    C = Dm // F
    nk = (2 * H + 1) * T
    f = lax.axis_index("fsdp")
    s = lax.axis_index("seq")
    z, y = lax.div(s, PAIR), lax.rem(s, PAIR)
    g, c = lax.div(f, PAIR), lax.rem(f, PAIR)
    partner = (f, z * PAIR + 1 - y)
    twin = (g * PAIR + 1 - c, s)

    def line(k):
        return (f, lax.rem(z + k, R) * PAIR + y)

    def across(k):
        return (lax.rem(g + k, G) * PAIR + c, s)

    barrier = pltpu.get_barrier_semaphore()
    peers = [partner, twin] + [line(k) for k in range(1, R)] + [across(k) for k in range(1, G)]
    for peer in peers:
        pl.semaphore_signal(barrier, inc=1, device_id=peer, device_id_type=pl.DeviceIdType.MESH)
    pl.semaphore_wait(barrier, len(peers))

    def remote(src, dst, send, recv, to):
        return pltpu.make_async_remote_copy(
            src_ref=src, dst_ref=dst, send_sem=send, recv_sem=recv,
            device_id=to, device_id_type=pl.DeviceIdType.MESH,
        )

    def cols(comp, j, half):
        return pl.ds(pl.multiple_of(comp * Dm + (PAIR * j + half) * cw, cw), cw)

    def place(comp, j, block):
        if comp == 0:
            return q_buf.at[j, pl.ds(pl.multiple_of(block * T, T), T), :]
        return kv_buf.at[j, comp - 1, pl.ds(pl.multiple_of((H + block) * T, T), T), :]

    def exchange(comp, j):
        return remote(
            qkv_ref.at[:, cols(comp, j, 1 - y)], place(comp, j, y),
            yx_s.at[comp, j], yx_r.at[comp, j], partner,
        )

    def arrived(comp, j):
        return remote(
            qkv_ref.at[:, cols(comp, j, 1 - y)], place(comp, j, 1 - y),
            yx_s.at[comp, j], yx_r.at[comp, j], partner,
        )

    def local(comp, j):
        return pltpu.make_async_copy(
            qkv_ref.at[:, cols(comp, j, y)], place(comp, j, y), loc.at[comp, j]
        )

    def halo(d, i, j):
        b, slot = (2 - H + i, i) if d == 0 else (i, H + 2 + i)
        to = (f, s + PAIR if d == 0 else s - PAIR)
        return remote(
            kv_buf.at[j, :, (H + b) * T : (H + b + 1) * T, :],
            kv_buf.at[j, :, slot * T : (slot + 1) * T, :],
            ha_s.at[d, i, j], ha_r.at[d, i, j], to,
        )

    sends = (z < R - 1, z > 0)
    comes = (z > 0, z < R - 1)

    def start_halos(j, own):
        for d in range(2):
            for i in range(H):
                b = 2 - H + i if d == 0 else i
                mine = (y == b) if own else (y != b)

                @pl.when(jnp.logical_and(mine, sends[d]))
                def _():
                    halo(d, i, j).start()

    def w_from(k):
        return lax.rem(z + R - k, R)

    def w_line(k):
        return remote(wbuf.at[f, z], wbuf.at[f, z], wz_s.at[k], wz_r.at[k], line(k))

    def w_line_in(k):
        at = wbuf.at[f, w_from(k)]
        return remote(at, at, wz_s.at[k], wz_r.at[k], line(k))

    def w_across(k, n):
        at = wbuf.at[f, w_from(k)]
        return remote(at, at, wx_s.at[k, n], wx_r.at[k, n], across(n))

    def w_across_in(k, n):
        at = wbuf.at[lax.rem(g + G - n, G) * PAIR + c, w_from(k)]
        return remote(at, at, wx_s.at[k, n], wx_r.at[k, n], across(n))

    def w_twin(k, n):
        at = wbuf.at[lax.rem(g + G - n, G) * PAIR + c, w_from(k)]
        return remote(at, at, wc_s.at[k, n], wc_r.at[k, n], twin)

    def w_twin_in(k, n):
        at = wbuf.at[lax.rem(g + G - n, G) * PAIR + 1 - c, w_from(k)]
        return remote(at, at, wc_s.at[k, n], wc_r.at[k, n], twin)

    for j in range(R):
        for comp in (1, 2):
            exchange(comp, j).start()
            local(comp, j).start()
    for j in range(R):
        exchange(0, j).start()
        local(0, j).start()

    new = (
        ema_decay * tea_ref[...].astype(jnp.float32)
        + (1.0 - ema_decay) * stu_ref[...].astype(jnp.float32)
    ).astype(jnp.bfloat16)
    new_ref[...] = new
    wbuf[f, z] = new
    for j in range(R):
        local(1, j).wait()
        local(2, j).wait()
        start_halos(j, True)
    for k in range(1, R):
        w_line(k).start()

    @pl.when(z == 0)
    def _():
        kv_buf[:, :, 0 : H * T, :] = jnp.zeros((R, 2, H * T, cw), jnp.bfloat16)

    @pl.when(z == R - 1)
    def _():
        kv_buf[:, :, (H + 2) * T :, :] = jnp.zeros((R, 2, H * T, cw), jnp.bfloat16)

    for b in range(2):
        first = z * (PAIR * T) + b * T
        rows = first + lax.broadcasted_iota(jnp.int32, (T, nk), 0)
        keys = first - H * T + lax.broadcasted_iota(jnp.int32, (T, nk), 1)
        row_segment = jnp.zeros((T, nk), jnp.int32)
        key_segment = jnp.where(jnp.logical_or(keys < 0, keys >= S * T), -1, 0)
        end = 0
        for n in range(len_ref.shape[1]):
            end = end + len_ref[0, n]
            row_segment = row_segment + (rows >= end).astype(jnp.int32)
            key_segment = key_segment + (keys >= end).astype(jnp.int32)
        outside = jnp.logical_or(keys < 0, keys >= S * T)
        same = jnp.logical_and(row_segment == key_segment, jnp.logical_not(outside))
        bias[b] = jnp.where(same, 0.0, masked_score)

    def forward(j, carry):
        arrived(1, j).wait_recv()
        arrived(2, j).wait_recv()
        start_halos(j, False)
        return carry

    lax.fori_loop(0, R, forward, 0)

    scale = log2_e / math.sqrt(hd)

    def attend(j, carry):
        @pl.when(j > 0)
        def _():
            w_line_in(j).wait_recv()

        for n in range(1, G):
            w_across(j, n).start()
        w_twin(j, 0).start()

        @pl.when(j > 0)
        def _():
            for n in range(1, G):
                w_across_in(j - 1, n).wait_recv()
                w_twin(j - 1, n).start()

        local(0, j).wait()
        arrived(0, j).wait_recv()
        for d in range(2):
            for i in range(H):

                @pl.when(comes[d])
                def _():
                    halo(d, i, j).wait_recv()

        head_of = lax.broadcasted_iota(jnp.int32, (T, cw), 1) // hd
        for b in range(2):
            query = q_buf[j, b * T : (b + 1) * T, :].astype(jnp.float32)
            key = kv_buf[j, 0, b * T : b * T + nk, :]
            value = kv_buf[j, 1, b * T : b * T + nk, :]
            stacked = jnp.concatenate(
                [jnp.where(head_of == h, query, 0.0).astype(jnp.bfloat16) for h in range(hp)], axis=0
            )
            scores = lax.dot_general(
                stacked, key, (((1,), (1,)), ((), ())), preferred_element_type=jnp.float32
            )
            scores = scores.reshape(hp, T, nk) * scale + bias[b][None]
            weights = jnp.exp2(scores - jnp.max(scores, axis=2, keepdims=True))
            total = jnp.sum(weights, axis=2, keepdims=True)
            summed = jnp.dot(
                weights.astype(jnp.bfloat16).reshape(hp * T, nk), value,
                preferred_element_type=jnp.float32,
            ).reshape(hp, T, cw) / total
            picked = summed[0]
            for h in range(1, hp):
                picked = jnp.where(head_of == h, summed[h], picked)
            mixed[j, b * T : (b + 1) * T, :] = picked.astype(jnp.bfloat16)
        return carry

    lax.fori_loop(0, R, attend, 0)

    for n in range(1, G):
        w_across_in(R - 1, n).wait_recv()
        w_twin(R - 1, n).start()

    def w_done(k, carry):
        for n in range(G):
            w_twin_in(k, n).wait_recv()
        return carry

    lax.fori_loop(0, R, w_done, 0)

    def part(block, col):
        total = jnp.zeros((T, C), jnp.float32)
        for j in range(R):
            total = total + jnp.dot(
                mixed[j, pl.ds(pl.multiple_of(block * T, T), T), :], wbuf[col, j],
                preferred_element_type=jnp.float32,
            )
        return total

    def give(col):
        return remote(psend.at[col], precv.at[col], pa_s.at[col], pa_r.at[col], partner)

    def give_part(col, carry):
        psend[col] = part(1 - y, col).astype(jnp.bfloat16)
        give(col).start()
        return carry

    def keep_part(col, carry):
        acc[col] = part(y, col)
        return carry

    lax.fori_loop(0, F, give_part, 0)
    lax.fori_loop(0, F, keep_part, 0)

    total = jnp.zeros((T, 1), jnp.float32)
    for col in range(F):
        give(col).wait_recv()
        branch = (acc[col] + precv[col].astype(jnp.float32)) * (1.0 / math.sqrt(Dm))
        summed = resid_ref[:, col * C : (col + 1) * C].astype(jnp.float32) + branch
        acc[col] = summed
        total = total + jnp.sum(summed, axis=1, keepdims=True)
    mean = total / Dm
    square = jnp.zeros((T, 1), jnp.float32)
    for col in range(F):
        centered = acc[col] - mean
        square = square + jnp.sum(centered * centered, axis=1, keepdims=True)
    gain = lax.rsqrt(square / Dm + norm_epsilon)
    for col in range(F):
        at = slice(col * C, (col + 1) * C)
        out_ref[:, at] = (earlier_ref[:, at] + (acc[col] - mean) * gain) * (1.0 / TOP_K)

    def drain(j, carry):
        for comp in range(3):
            exchange(comp, j).wait_send()
        for d in range(2):
            for i in range(H):

                @pl.when(sends[d])
                def _():
                    halo(d, i, j).wait_send()

        @pl.when(j > 0)
        def _():
            w_line(j).wait_send()

        for n in range(1, G):
            w_across(j, n).wait_send()
        for n in range(G):
            w_twin(j, n).wait_send()
        return carry

    lax.fori_loop(0, R, drain, 0)

    def drain_parts(col, carry):
        give(col).wait_send()
        return carry

    lax.fori_loop(0, F, drain_parts, 0)


def segment_ids(utt_lengths, frames):
    order = jnp.arange(utt_lengths.shape[0])
    utt_ends = jnp.sum(jnp.where(order[None, :] <= order[:, None], utt_lengths[None, :], 0), axis=1)
    places = jnp.arange(frames, dtype=jnp.int32)
    return jnp.sum((places[:, None] >= utt_ends[None, :]).astype(jnp.int32), axis=1)


def attend_window(stacked, segment):
    frames = stacked.shape[0]
    longest = frames // 8
    rows_block = min(512, frames)
    key_span = min(frames, rows_block + 2 * longest)
    inverse_root = 1.0 / math.sqrt(stacked.shape[-1])
    queries = stacked[:, 0]
    keys_all = stacked[:, 1]
    values_all = stacked[:, 2]

    def one_block(row_start):
        key_start = jnp.clip(row_start - longest, 0, frames - key_span)
        block_queries = lax.dynamic_slice_in_dim(queries, row_start, rows_block, 0)
        query_segment = lax.dynamic_slice_in_dim(segment, row_start, rows_block, 0)
        block_keys = lax.dynamic_slice_in_dim(keys_all, key_start, key_span, 0)
        block_values = lax.dynamic_slice_in_dim(values_all, key_start, key_span, 0)
        key_segment = lax.dynamic_slice_in_dim(segment, key_start, key_span, 0)
        scores = (
            jnp.einsum(
                "qhd,khd->hqk", block_queries, block_keys, preferred_element_type=jnp.float32
            )
            * inverse_root
        )
        allowed = (query_segment[:, None] == key_segment[None, :])[None]
        scores = jnp.where(allowed, scores, masked_score)
        row_max = jnp.max(scores, axis=2, keepdims=True)
        weights = jnp.exp(scores - row_max)
        row_total = jnp.sum(weights, axis=2)
        summed = jnp.einsum(
            "hqk,khd->qhd",
            weights.astype(jnp.bfloat16),
            block_values,
            preferred_element_type=jnp.float32,
        )
        return (summed / jnp.transpose(row_total)[:, :, None]).astype(jnp.bfloat16)

    starts = jnp.arange(frames // rows_block, dtype=jnp.int32) * rows_block
    outputs = lax.map(one_block, starts)
    return outputs.reshape(frames, stacked.shape[2], stacked.shape[3])


def spread(qkv, resid, earlier, lengths, teacher_out, student_out):
    teacher_new = (
        ema_decay * teacher_out.astype(jnp.float32)
        + (1.0 - ema_decay) * student_out.astype(jnp.float32)
    ).astype(jnp.bfloat16)
    tokens = qkv.shape[1]
    groups = lax.axis_size("seq")
    frames = tokens * groups
    segment = segment_ids(lengths[0], frames)
    own_heads = qkv[0].reshape(tokens, 3, groups, HEADS // groups, HEAD_DIM)
    attended = attend_window(
        lax.all_to_all(own_heads, "seq", split_axis=2, concat_axis=0, tiled=True)[:, :, 0], segment
    )
    regathered = lax.all_to_all(attended[:, None], "seq", split_axis=0, concat_axis=1, tiled=True)
    mixed_rows = regathered.reshape(tokens, HEADS * HEAD_DIM)
    full_rows = lax.all_gather(teacher_new, "seq", axis=0, tiled=True)
    branch = jnp.dot(
        mixed_rows,
        lax.all_gather(full_rows, "fsdp", axis=1, tiled=True),
        preferred_element_type=jnp.float32,
    )
    branch = branch / math.sqrt(HEADS * HEAD_DIM)
    summed = resid[0].astype(jnp.float32) + branch
    centered = summed - jnp.mean(summed, axis=1, keepdims=True)
    normed = centered * lax.rsqrt(
        jnp.mean(centered * centered, axis=1, keepdims=True) + norm_epsilon
    )
    targets = ((earlier[0] + normed) / TOP_K)[None]
    return (targets, teacher_new)


def shards(F, S, qkv, resid, earlier, lengths, teacher_out, student_out):
    T, width = qkv.shape[1:]
    Dm = resid.shape[2]
    longest = T * S // 8
    H = -(-(longest - 1) // T)
    R, G, C, cw = S // PAIR, F // PAIR, Dm // F, Dm // S
    if S % PAIR or F % PAIR or H > PAIR or cw % 128 or C % 128 or T % 16:
        return spread(qkv, resid, earlier, lengths, teacher_out, student_out)
    nk = (2 * H + 1) * T
    vmem = pl.BlockSpec(memory_space=pltpu.VMEM)
    dma = pltpu.SemaphoreType.DMA
    targets, teacher_new = pl.pallas_call(
        functools.partial(body, F, S, H),
        out_shape=(
            jax.ShapeDtypeStruct((T, Dm), jnp.float32),
            jax.ShapeDtypeStruct(teacher_out.shape, jnp.bfloat16),
        ),
        in_specs=[pl.BlockSpec(memory_space=pltpu.SMEM)] + [vmem] * 5,
        out_specs=(vmem, vmem),
        scratch_shapes=[
            pltpu.VMEM((R, PAIR * T, cw), jnp.bfloat16),
            pltpu.VMEM((R, 2, (PAIR + 2 * H) * T, cw), jnp.bfloat16),
            pltpu.VMEM((R, PAIR * T, cw), jnp.bfloat16),
            pltpu.VMEM((F, R) + teacher_out.shape, jnp.bfloat16),
            pltpu.VMEM((PAIR, T, nk), jnp.float32),
            pltpu.VMEM((F, T, C), jnp.bfloat16),
            pltpu.VMEM((F, T, C), jnp.bfloat16),
            pltpu.VMEM((F, T, C), jnp.float32),
            dma((3, R)), dma((3, R)), dma((3, R)),
            dma((2, H, R)), dma((2, H, R)),
            dma((R,)), dma((R,)),
            dma((R, G)), dma((R, G)),
            dma((R, G)), dma((R, G)),
            dma((F,)), dma((F,)),
        ],
        compiler_params=pltpu.CompilerParams(
            collective_id=0, has_side_effects=True, vmem_limit_bytes=48 * 2**20
        ),
        cost_estimate=pl.CostEstimate(
            flops=4 * T * nk * Dm + 2 * T * Dm * Dm, bytes_accessed=2 * T * width + 14 * T * Dm,
            transcendentals=HEADS * T * nk,
        ),
    )(lengths, qkv[0], resid[0], earlier[0], teacher_out, student_out)
    return (targets[None], teacher_new)


def solution(mesh):
    placed = (
        P("fsdp", "seq", None),
        P("fsdp", "seq", None),
        P("fsdp", "seq", None),
        P("fsdp", None),
        P("seq", "fsdp"),
        P("seq", "fsdp"),
    )
    return jax.shard_map(
        functools.partial(shards, mesh.shape["fsdp"], mesh.shape["seq"]),
        mesh=mesh,
        in_specs=placed,
        out_specs=(P("fsdp", "seq", None), P("seq", "fsdp")),
        check_vma=False,
    )
```

```python
import functools
import math

import jax
import jax.numpy as jnp
from jax import lax
from jax.experimental import pallas as pl
from jax.experimental.pallas import tpu as pltpu
from jax.sharding import PartitionSpec as P

HEADS = 32
HEAD_DIM = 64
TOP_K = 8
PAIR = 2

ema_decay = 0.9
norm_epsilon = 1e-05
masked_score = -1e30
log2_e = math.log2(math.e)


def body(
    F, S, H,
    len_ref, qkv_ref, resid_hbm, earlier_hbm, tea_hbm, stu_hbm,
    out_ref, new_ref,
    resid_ref, earlier_ref, tea_ref, stu_ref, in_sem,
    q_buf, kv_buf, mixed, wbuf, bias, psend, precv, acc,
    yx_s, yx_r, loc, ha_s, ha_r, wz_s, wz_r, wx_s, wx_r, wc_s, wc_r, pa_s, pa_r,
):
    T = qkv_ref.shape[0]
    Dm = resid_hbm.shape[1]
    cw = Dm // S
    hd = Dm // HEADS
    hp = cw // hd
    R = S // PAIR
    G = F // PAIR
    C = Dm // F
    nk = (2 * H + 1) * T
    f = lax.axis_index("fsdp")
    s = lax.axis_index("seq")
    z, y = lax.div(s, PAIR), lax.rem(s, PAIR)
    g, c = lax.div(f, PAIR), lax.rem(f, PAIR)
    partner = (f, z * PAIR + 1 - y)
    twin = (g * PAIR + 1 - c, s)

    def line(k):
        return (f, lax.rem(z + k, R) * PAIR + y)

    def across(k):
        return (lax.rem(g + k, G) * PAIR + c, s)

    def cols(comp, j, half):
        return pl.ds(pl.multiple_of(comp * Dm + (PAIR * j + half) * cw, cw), cw)

    def place(comp, j, block):
        if comp == 0:
            return q_buf.at[j, pl.ds(pl.multiple_of(block * T, T), T), :]
        return kv_buf.at[j, comp - 1, pl.ds(pl.multiple_of((H + block) * T, T), T), :]

    def local(comp, j):
        return pltpu.make_async_copy(
            qkv_ref.at[:, cols(comp, j, y)], place(comp, j, y), loc.at[comp, j]
        )

    staged = [
        pltpu.make_async_copy(src, dst, in_sem.at[n])
        for n, (src, dst) in enumerate(
            ((tea_hbm, tea_ref), (stu_hbm, stu_ref), (resid_hbm, resid_ref), (earlier_hbm, earlier_ref))
        )
    ]
    for j in range(R):
        local(1, j).start()
        local(2, j).start()
    staged[0].start()
    staged[1].start()
    for j in range(R):
        local(0, j).start()

    barrier = pltpu.get_barrier_semaphore()
    peers = [partner, twin] + [line(k) for k in range(1, R)] + [across(k) for k in range(1, G)]
    for peer in peers:
        pl.semaphore_signal(barrier, inc=1, device_id=peer, device_id_type=pl.DeviceIdType.MESH)
    pl.semaphore_wait(barrier, len(peers))

    def remote(src, dst, send, recv, to):
        return pltpu.make_async_remote_copy(
            src_ref=src, dst_ref=dst, send_sem=send, recv_sem=recv,
            device_id=to, device_id_type=pl.DeviceIdType.MESH,
        )

    def exchange(comp, j):
        return remote(
            qkv_ref.at[:, cols(comp, j, 1 - y)], place(comp, j, y),
            yx_s.at[comp, j], yx_r.at[comp, j], partner,
        )

    def arrived(comp, j):
        return remote(
            qkv_ref.at[:, cols(comp, j, 1 - y)], place(comp, j, 1 - y),
            yx_s.at[comp, j], yx_r.at[comp, j], partner,
        )

    def halo(d, i, j):
        b, slot = (2 - H + i, i) if d == 0 else (i, H + 2 + i)
        to = (f, s + PAIR if d == 0 else s - PAIR)
        return remote(
            kv_buf.at[j, :, (H + b) * T : (H + b + 1) * T, :],
            kv_buf.at[j, :, slot * T : (slot + 1) * T, :],
            ha_s.at[d, i, j], ha_r.at[d, i, j], to,
        )

    sends = (z < R - 1, z > 0)
    comes = (z > 0, z < R - 1)

    def start_halos(j, own):
        for d in range(2):
            for i in range(H):
                b = 2 - H + i if d == 0 else i
                mine = (y == b) if own else (y != b)

                @pl.when(jnp.logical_and(mine, sends[d]))
                def _():
                    halo(d, i, j).start()

    def w_from(k):
        return lax.rem(z + R - k, R)

    def w_line(k):
        return remote(wbuf.at[f, z], wbuf.at[f, z], wz_s.at[k], wz_r.at[k], line(k))

    def w_line_in(k):
        at = wbuf.at[f, w_from(k)]
        return remote(at, at, wz_s.at[k], wz_r.at[k], line(k))

    def w_across(k, n):
        at = wbuf.at[f, w_from(k)]
        return remote(at, at, wx_s.at[k, n], wx_r.at[k, n], across(n))

    def w_across_in(k, n):
        at = wbuf.at[lax.rem(g + G - n, G) * PAIR + c, w_from(k)]
        return remote(at, at, wx_s.at[k, n], wx_r.at[k, n], across(n))

    def w_twin(k, n):
        at = wbuf.at[lax.rem(g + G - n, G) * PAIR + c, w_from(k)]
        return remote(at, at, wc_s.at[k, n], wc_r.at[k, n], twin)

    def w_twin_in(k, n):
        at = wbuf.at[lax.rem(g + G - n, G) * PAIR + 1 - c, w_from(k)]
        return remote(at, at, wc_s.at[k, n], wc_r.at[k, n], twin)

    for j in range(R):
        exchange(1, j).start()
        exchange(2, j).start()
        if j > 0:
            exchange(0, j - 1).start()
    exchange(0, R - 1).start()

    for j in range(R):
        local(1, j).wait()
        local(2, j).wait()
        start_halos(j, True)

    staged[0].wait()
    staged[1].wait()
    new = (
        ema_decay * tea_ref[...].astype(jnp.float32)
        + (1.0 - ema_decay) * stu_ref[...].astype(jnp.float32)
    ).astype(jnp.bfloat16)
    new_ref[...] = new
    wbuf[f, z] = new
    for n in range(1, G):
        w_across(0, n).start()
    w_twin(0, 0).start()
    for k in range(1, R):
        w_line(k).start()
    staged[2].start()
    staged[3].start()

    @pl.when(z == 0)
    def _():
        kv_buf[:, :, 0 : H * T, :] = jnp.zeros((R, 2, H * T, cw), jnp.bfloat16)

    @pl.when(z == R - 1)
    def _():
        kv_buf[:, :, (H + 2) * T :, :] = jnp.zeros((R, 2, H * T, cw), jnp.bfloat16)

    for b in range(2):
        first = z * (PAIR * T) + b * T
        rows = first + lax.broadcasted_iota(jnp.int32, (T, nk), 0)
        keys = first - H * T + lax.broadcasted_iota(jnp.int32, (T, nk), 1)
        row_segment = jnp.zeros((T, nk), jnp.int32)
        key_segment = jnp.where(jnp.logical_or(keys < 0, keys >= S * T), -1, 0)
        end = 0
        for n in range(len_ref.shape[1]):
            end = end + len_ref[0, n]
            row_segment = row_segment + (rows >= end).astype(jnp.int32)
            key_segment = key_segment + (keys >= end).astype(jnp.int32)
        outside = jnp.logical_or(keys < 0, keys >= S * T)
        same = jnp.logical_and(row_segment == key_segment, jnp.logical_not(outside))
        bias[b] = jnp.where(same, 0.0, masked_score)

    def forward(j):
        arrived(1, j).wait_recv()
        arrived(2, j).wait_recv()
        start_halos(j, False)

    forward(0)

    scale = log2_e / math.sqrt(hd)

    def attend(j, carry):
        @pl.when(j < R - 1)
        def _():
            forward(j + 1)
            w_line_in(j + 1).wait_recv()
            for n in range(1, G):
                w_across(j + 1, n).start()
            w_twin(j + 1, 0).start()

        @pl.when(j > 0)
        def _():
            for n in range(1, G):
                w_across_in(j - 1, n).wait_recv()
                w_twin(j - 1, n).start()

        local(0, j).wait()
        arrived(0, j).wait_recv()
        for d in range(2):
            for i in range(H):

                @pl.when(comes[d])
                def _():
                    halo(d, i, j).wait_recv()

        head_of = lax.broadcasted_iota(jnp.int32, (T, cw), 1) // hd
        for b in range(2):
            query = q_buf[j, b * T : (b + 1) * T, :].astype(jnp.float32)
            key = kv_buf[j, 0, b * T : b * T + nk, :]
            value = kv_buf[j, 1, b * T : b * T + nk, :]
            stacked = jnp.concatenate(
                [jnp.where(head_of == h, query, 0.0).astype(jnp.bfloat16) for h in range(hp)], axis=0
            )
            scores = lax.dot_general(
                stacked, key, (((1,), (1,)), ((), ())), preferred_element_type=jnp.float32
            )
            scores = scores.reshape(hp, T, nk) * scale + bias[b][None]
            weights = jnp.exp2(scores - jnp.max(scores, axis=2, keepdims=True))
            total = jnp.sum(weights, axis=2, keepdims=True)
            summed = jnp.dot(
                weights.astype(jnp.bfloat16).reshape(hp * T, nk), value,
                preferred_element_type=jnp.float32,
            ).reshape(hp, T, cw) / total
            picked = summed[0]
            for h in range(1, hp):
                picked = jnp.where(head_of == h, summed[h], picked)
            mixed[j, b * T : (b + 1) * T, :] = picked.astype(jnp.bfloat16)
        return carry

    lax.fori_loop(0, R, attend, 0)

    def part(block, col):
        total = jnp.zeros((T, C), jnp.float32)
        for j in range(R):
            total = total + jnp.dot(
                mixed[j, pl.ds(pl.multiple_of(block * T, T), T), :], wbuf[col, j],
                preferred_element_type=jnp.float32,
            )
        return total

    def give(col):
        return remote(psend.at[col], precv.at[col], pa_s.at[col], pa_r.at[col], partner)

    def give_part(col):
        psend[col] = part(1 - y, col).astype(jnp.bfloat16)
        give(col).start()

    def twin_part(n):
        for k in range(R):
            w_twin_in(k, n).wait_recv()
        give_part(lax.rem(g + G - n, G) * PAIR + 1 - c)

    give_part(f)
    twin_part(0)
    for n in range(1, G):
        w_across_in(R - 1, n).wait_recv()
        w_twin(R - 1, n).start()
        give_part(lax.rem(g + G - n, G) * PAIR + c)
    for n in range(1, G):
        twin_part(n)

    def keep_part(col, carry):
        acc[col] = part(y, col)
        return carry

    lax.fori_loop(0, F, keep_part, 0)

    staged[2].wait()
    staged[3].wait()
    total = jnp.zeros((T, 1), jnp.float32)
    for col in range(F):
        give(col).wait_recv()
        branch = (acc[col] + precv[col].astype(jnp.float32)) * (1.0 / math.sqrt(Dm))
        summed = resid_ref[:, col * C : (col + 1) * C].astype(jnp.float32) + branch
        acc[col] = summed
        total = total + jnp.sum(summed, axis=1, keepdims=True)
    mean = total / Dm
    square = jnp.zeros((T, 1), jnp.float32)
    for col in range(F):
        centered = acc[col] - mean
        square = square + jnp.sum(centered * centered, axis=1, keepdims=True)
    gain = lax.rsqrt(square / Dm + norm_epsilon)
    for col in range(F):
        at = slice(col * C, (col + 1) * C)
        out_ref[:, at] = (earlier_ref[:, at] + (acc[col] - mean) * gain) * (1.0 / TOP_K)

    def drain(j, carry):
        for comp in range(3):
            exchange(comp, j).wait_send()
        for d in range(2):
            for i in range(H):

                @pl.when(sends[d])
                def _():
                    halo(d, i, j).wait_send()

        @pl.when(j > 0)
        def _():
            w_line(j).wait_send()

        for n in range(1, G):
            w_across(j, n).wait_send()
        for n in range(G):
            w_twin(j, n).wait_send()
        return carry

    lax.fori_loop(0, R, drain, 0)

    def drain_parts(col, carry):
        give(col).wait_send()
        return carry

    lax.fori_loop(0, F, drain_parts, 0)


def segment_ids(utt_lengths, frames):
    order = jnp.arange(utt_lengths.shape[0])
    utt_ends = jnp.sum(jnp.where(order[None, :] <= order[:, None], utt_lengths[None, :], 0), axis=1)
    places = jnp.arange(frames, dtype=jnp.int32)
    return jnp.sum((places[:, None] >= utt_ends[None, :]).astype(jnp.int32), axis=1)


def attend_window(stacked, segment):
    frames = stacked.shape[0]
    longest = frames // 8
    rows_block = min(512, frames)
    key_span = min(frames, rows_block + 2 * longest)
    inverse_root = 1.0 / math.sqrt(stacked.shape[-1])
    queries = stacked[:, 0]
    keys_all = stacked[:, 1]
    values_all = stacked[:, 2]

    def one_block(row_start):
        key_start = jnp.clip(row_start - longest, 0, frames - key_span)
        block_queries = lax.dynamic_slice_in_dim(queries, row_start, rows_block, 0)
        query_segment = lax.dynamic_slice_in_dim(segment, row_start, rows_block, 0)
        block_keys = lax.dynamic_slice_in_dim(keys_all, key_start, key_span, 0)
        block_values = lax.dynamic_slice_in_dim(values_all, key_start, key_span, 0)
        key_segment = lax.dynamic_slice_in_dim(segment, key_start, key_span, 0)
        scores = (
            jnp.einsum(
                "qhd,khd->hqk", block_queries, block_keys, preferred_element_type=jnp.float32
            )
            * inverse_root
        )
        allowed = (query_segment[:, None] == key_segment[None, :])[None]
        scores = jnp.where(allowed, scores, masked_score)
        row_max = jnp.max(scores, axis=2, keepdims=True)
        weights = jnp.exp(scores - row_max)
        row_total = jnp.sum(weights, axis=2)
        summed = jnp.einsum(
            "hqk,khd->qhd",
            weights.astype(jnp.bfloat16),
            block_values,
            preferred_element_type=jnp.float32,
        )
        return (summed / jnp.transpose(row_total)[:, :, None]).astype(jnp.bfloat16)

    starts = jnp.arange(frames // rows_block, dtype=jnp.int32) * rows_block
    outputs = lax.map(one_block, starts)
    return outputs.reshape(frames, stacked.shape[2], stacked.shape[3])


def spread(qkv, resid, earlier, lengths, teacher_out, student_out):
    teacher_new = (
        ema_decay * teacher_out.astype(jnp.float32)
        + (1.0 - ema_decay) * student_out.astype(jnp.float32)
    ).astype(jnp.bfloat16)
    tokens = qkv.shape[1]
    groups = lax.axis_size("seq")
    frames = tokens * groups
    segment = segment_ids(lengths[0], frames)
    own_heads = qkv[0].reshape(tokens, 3, groups, HEADS // groups, HEAD_DIM)
    attended = attend_window(
        lax.all_to_all(own_heads, "seq", split_axis=2, concat_axis=0, tiled=True)[:, :, 0], segment
    )
    regathered = lax.all_to_all(attended[:, None], "seq", split_axis=0, concat_axis=1, tiled=True)
    mixed_rows = regathered.reshape(tokens, HEADS * HEAD_DIM)
    full_rows = lax.all_gather(teacher_new, "seq", axis=0, tiled=True)
    branch = jnp.dot(
        mixed_rows,
        lax.all_gather(full_rows, "fsdp", axis=1, tiled=True),
        preferred_element_type=jnp.float32,
    )
    branch = branch / math.sqrt(HEADS * HEAD_DIM)
    summed = resid[0].astype(jnp.float32) + branch
    centered = summed - jnp.mean(summed, axis=1, keepdims=True)
    normed = centered * lax.rsqrt(
        jnp.mean(centered * centered, axis=1, keepdims=True) + norm_epsilon
    )
    targets = ((earlier[0] + normed) / TOP_K)[None]
    return (targets, teacher_new)


def shards(F, S, qkv, resid, earlier, lengths, teacher_out, student_out):
    T, width = qkv.shape[1:]
    Dm = resid.shape[2]
    longest = T * S // 8
    H = -(-(longest - 1) // T)
    R, G, C, cw = S // PAIR, F // PAIR, Dm // F, Dm // S
    if S % PAIR or F % PAIR or H > PAIR or cw % 128 or C % 128 or T % 16:
        return spread(qkv, resid, earlier, lengths, teacher_out, student_out)
    nk = (2 * H + 1) * T
    vmem = pl.BlockSpec(memory_space=pltpu.VMEM)
    hbm = pl.BlockSpec(memory_space=pltpu.HBM)
    dma = pltpu.SemaphoreType.DMA
    targets, teacher_new = pl.pallas_call(
        functools.partial(body, F, S, H),
        out_shape=(
            jax.ShapeDtypeStruct((T, Dm), jnp.float32),
            jax.ShapeDtypeStruct(teacher_out.shape, jnp.bfloat16),
        ),
        in_specs=[pl.BlockSpec(memory_space=pltpu.SMEM)] + [hbm] * 5,
        out_specs=(vmem, vmem),
        scratch_shapes=[
            pltpu.VMEM((T, Dm), resid.dtype),
            pltpu.VMEM((T, Dm), earlier.dtype),
            pltpu.VMEM(teacher_out.shape, teacher_out.dtype),
            pltpu.VMEM(student_out.shape, student_out.dtype),
            dma((4,)),
            pltpu.VMEM((R, PAIR * T, cw), jnp.bfloat16),
            pltpu.VMEM((R, 2, (PAIR + 2 * H) * T, cw), jnp.bfloat16),
            pltpu.VMEM((R, PAIR * T, cw), jnp.bfloat16),
            pltpu.VMEM((F, R) + teacher_out.shape, jnp.bfloat16),
            pltpu.VMEM((PAIR, T, nk), jnp.float32),
            pltpu.VMEM((F, T, C), jnp.bfloat16),
            pltpu.VMEM((F, T, C), jnp.bfloat16),
            pltpu.VMEM((F, T, C), jnp.float32),
            dma((3, R)), dma((3, R)), dma((3, R)),
            dma((2, H, R)), dma((2, H, R)),
            dma((R,)), dma((R,)),
            dma((R, G)), dma((R, G)),
            dma((R, G)), dma((R, G)),
            dma((F,)), dma((F,)),
        ],
        compiler_params=pltpu.CompilerParams(
            collective_id=0, has_side_effects=True, vmem_limit_bytes=63 * 2**20
        ),
        cost_estimate=pl.CostEstimate(
            flops=4 * T * nk * Dm + 2 * T * Dm * Dm, bytes_accessed=2 * T * width + 14 * T * Dm,
            transcendentals=HEADS * T * nk,
        ),
    )(lengths, qkv[0], resid[0], earlier[0], teacher_out, student_out)
    return (targets[None], teacher_new)


def solution(mesh):
    placed = (
        P("fsdp", "seq", None),
        P("fsdp", "seq", None),
        P("fsdp", "seq", None),
        P("fsdp", None),
        P("seq", "fsdp"),
        P("seq", "fsdp"),
    )
    return jax.shard_map(
        functools.partial(shards, mesh.shape["fsdp"], mesh.shape["seq"]),
        mesh=mesh,
        in_specs=placed,
        out_specs=(P("fsdp", "seq", None), P("seq", "fsdp")),
        check_vma=False,
    )
```

```python
import functools
import math

import jax
import jax.numpy as jnp
from jax import lax
from jax.experimental import pallas as pl
from jax.experimental.pallas import tpu as pltpu
from jax.sharding import PartitionSpec as P

HEADS = 32
HEAD_DIM = 64
TOP_K = 8
PAIR = 2

ema_decay = 0.9
norm_epsilon = 1e-05
masked_score = -1e30
log2_e = math.log2(math.e)


def body(
    F, S, H,
    len_ref, qkv_ref, resid_hbm, earlier_hbm, tea_hbm, stu_hbm,
    out_ref, new_ref,
    resid_ref, earlier_ref, tea_ref, stu_ref, in_sem,
    q_buf, kv_buf, mixed, wbuf, bias, psend, precv, acc,
    yx_s, yx_r, loc, ha_s, ha_r, wz_s, wz_r, wx_s, wx_r, wc_s, wc_r, pa_s, pa_r,
):
    T = qkv_ref.shape[0]
    Dm = resid_hbm.shape[1]
    cw = Dm // S
    hd = Dm // HEADS
    hp = cw // hd
    R = S // PAIR
    G = F // PAIR
    C = Dm // F
    nk = (2 * H + 1) * T
    f = lax.axis_index("fsdp")
    s = lax.axis_index("seq")
    z, y = lax.div(s, PAIR), lax.rem(s, PAIR)
    g, c = lax.div(f, PAIR), lax.rem(f, PAIR)
    partner = (f, z * PAIR + 1 - y)
    twin = (g * PAIR + 1 - c, s)

    def line(k):
        return (f, lax.rem(z + k, R) * PAIR + y)

    def across(k):
        return (lax.rem(g + k, G) * PAIR + c, s)

    def cols(comp, j, half):
        return pl.ds(pl.multiple_of(comp * Dm + (PAIR * j + half) * cw, cw), cw)

    def place(comp, j, block):
        if comp == 0:
            return q_buf.at[j, pl.ds(pl.multiple_of(block * T, T), T), :]
        return kv_buf.at[j, comp - 1, pl.ds(pl.multiple_of((H + block) * T, T), T), :]

    def local(comp, j):
        return pltpu.make_async_copy(
            qkv_ref.at[:, cols(comp, j, y)], place(comp, j, y), loc.at[comp, j]
        )

    staged = [
        pltpu.make_async_copy(src, dst, in_sem.at[n])
        for n, (src, dst) in enumerate(
            ((tea_hbm, tea_ref), (stu_hbm, stu_ref), (resid_hbm, resid_ref), (earlier_hbm, earlier_ref))
        )
    ]
    for j in range(R):
        local(1, j).start()
        local(2, j).start()
    staged[0].start()
    staged[1].start()
    for j in range(R):
        local(0, j).start()

    barrier = pltpu.get_barrier_semaphore()
    peers = [partner, twin] + [line(k) for k in range(1, R)] + [across(k) for k in range(1, G)]
    for peer in peers:
        pl.semaphore_signal(barrier, inc=1, device_id=peer, device_id_type=pl.DeviceIdType.MESH)
    pl.semaphore_wait(barrier, len(peers))

    def remote(src, dst, send, recv, to):
        return pltpu.make_async_remote_copy(
            src_ref=src, dst_ref=dst, send_sem=send, recv_sem=recv,
            device_id=to, device_id_type=pl.DeviceIdType.MESH,
        )

    def exchange(comp, j):
        return remote(
            qkv_ref.at[:, cols(comp, j, 1 - y)], place(comp, j, y),
            yx_s.at[comp, j], yx_r.at[comp, j], partner,
        )

    def arrived(comp, j):
        return remote(
            qkv_ref.at[:, cols(comp, j, 1 - y)], place(comp, j, 1 - y),
            yx_s.at[comp, j], yx_r.at[comp, j], partner,
        )

    def halo(d, i, j):
        b, slot = (2 - H + i, i) if d == 0 else (i, H + 2 + i)
        to = (f, s + PAIR if d == 0 else s - PAIR)
        return remote(
            kv_buf.at[j, :, (H + b) * T : (H + b + 1) * T, :],
            kv_buf.at[j, :, slot * T : (slot + 1) * T, :],
            ha_s.at[d, i, j], ha_r.at[d, i, j], to,
        )

    sends = (z < R - 1, z > 0)
    comes = (z > 0, z < R - 1)

    def start_halos(j, own):
        for d in range(2):
            for i in range(H):
                b = 2 - H + i if d == 0 else i
                mine = (y == b) if own else (y != b)

                @pl.when(jnp.logical_and(mine, sends[d]))
                def _():
                    halo(d, i, j).start()

    def w_from(k):
        return lax.rem(z + R - k, R)

    def w_line(k):
        return remote(wbuf.at[f, z], wbuf.at[f, z], wz_s.at[k], wz_r.at[k], line(k))

    def w_line_in(k):
        at = wbuf.at[f, w_from(k)]
        return remote(at, at, wz_s.at[k], wz_r.at[k], line(k))

    def w_across(k, n):
        at = wbuf.at[f, w_from(k)]
        return remote(at, at, wx_s.at[k, n], wx_r.at[k, n], across(n))

    def w_across_in(k, n):
        at = wbuf.at[lax.rem(g + G - n, G) * PAIR + c, w_from(k)]
        return remote(at, at, wx_s.at[k, n], wx_r.at[k, n], across(n))

    def w_twin(k, n):
        at = wbuf.at[lax.rem(g + G - n, G) * PAIR + c, w_from(k)]
        return remote(at, at, wc_s.at[k, n], wc_r.at[k, n], twin)

    def w_twin_in(k, n):
        at = wbuf.at[lax.rem(g + G - n, G) * PAIR + 1 - c, w_from(k)]
        return remote(at, at, wc_s.at[k, n], wc_r.at[k, n], twin)

    for j in range(R):
        exchange(1, j).start()
        exchange(2, j).start()
        if j > 0:
            exchange(0, j - 1).start()
    exchange(0, R - 1).start()

    for j in range(R):
        local(1, j).wait()
        local(2, j).wait()
        start_halos(j, True)

    staged[0].wait()
    staged[1].wait()
    new = (
        ema_decay * tea_ref[...].astype(jnp.float32)
        + (1.0 - ema_decay) * stu_ref[...].astype(jnp.float32)
    ).astype(jnp.bfloat16)
    new_ref[...] = new
    wbuf[f, z] = new
    for n in range(1, G):
        w_across(0, n).start()
    w_twin(0, 0).start()
    for k in range(1, R):
        w_line(k).start()
    staged[2].start()
    staged[3].start()

    @pl.when(z == 0)
    def _():
        kv_buf[:, :, 0 : H * T, :] = jnp.zeros((R, 2, H * T, cw), jnp.bfloat16)

    @pl.when(z == R - 1)
    def _():
        kv_buf[:, :, (H + 2) * T :, :] = jnp.zeros((R, 2, H * T, cw), jnp.bfloat16)

    for b in range(2):
        first = z * (PAIR * T) + b * T
        rows = first + lax.broadcasted_iota(jnp.int32, (T, nk), 0)
        keys = first - H * T + lax.broadcasted_iota(jnp.int32, (T, nk), 1)
        row_segment = jnp.zeros((T, nk), jnp.int32)
        key_segment = jnp.where(jnp.logical_or(keys < 0, keys >= S * T), -1, 0)
        end = 0
        for n in range(len_ref.shape[1]):
            end = end + len_ref[0, n]
            row_segment = row_segment + (rows >= end).astype(jnp.int32)
            key_segment = key_segment + (keys >= end).astype(jnp.int32)
        outside = jnp.logical_or(keys < 0, keys >= S * T)
        same = jnp.logical_and(row_segment == key_segment, jnp.logical_not(outside))
        bias[b] = jnp.where(same, 0.0, masked_score)

    def forward(j):
        arrived(1, j).wait_recv()
        arrived(2, j).wait_recv()
        start_halos(j, False)

    forward(0)

    scale = log2_e / math.sqrt(hd)

    def gather(j):
        @pl.when(j < R - 1)
        def _():
            forward(j + 1)
            w_line_in(j + 1).wait_recv()
            for n in range(1, G):
                w_across(j + 1, n).start()
            w_twin(j + 1, 0).start()

        @pl.when(j > 0)
        def _():
            for n in range(1, G):
                w_across_in(j - 1, n).wait_recv()
                w_twin(j - 1, n).start()

        local(0, j).wait()
        arrived(0, j).wait_recv()
        for d in range(2):
            for i in range(H):

                @pl.when(comes[d])
                def _():
                    halo(d, i, j).wait_recv()

    head_of = lax.broadcasted_iota(jnp.int32, (T, cw), 1) // hd

    def attend(j, b):
        at = pl.ds(pl.multiple_of(b * T, T), T)
        span = pl.ds(pl.multiple_of(b * T, T), nk)
        query = q_buf[j, at, :].astype(jnp.float32)
        stacked = jnp.concatenate(
            [jnp.where(head_of == h, query, 0.0).astype(jnp.bfloat16) for h in range(hp)], axis=0
        )
        scores = lax.dot_general(
            stacked, kv_buf[j, 0, span, :], (((1,), (1,)), ((), ())),
            preferred_element_type=jnp.float32,
        )
        scores = scores.reshape(hp, T, nk) * scale + bias[b][None]
        weights = jnp.exp2(scores - jnp.max(scores, axis=2, keepdims=True))
        total = jnp.sum(weights, axis=2, keepdims=True)
        summed = jnp.dot(
            weights.astype(jnp.bfloat16).reshape(hp * T, nk), kv_buf[j, 1, span, :],
            preferred_element_type=jnp.float32,
        ).reshape(hp, T, cw)
        picked, below = summed[0], total[0]
        for h in range(1, hp):
            picked = jnp.where(head_of == h, summed[h], picked)
            below = jnp.where(head_of == h, total[h], below)
        mixed[j, at, :] = (picked / below).astype(jnp.bfloat16)

    def attend_partner(j, carry):
        gather(j)
        attend(j, 1 - y)
        return carry

    def attend_own(j, carry):
        attend(j, y)
        return carry

    lax.fori_loop(0, R, attend_partner, 0)

    def part(block, col):
        total = jnp.zeros((T, C), jnp.float32)
        for j in range(R):
            total = total + jnp.dot(
                mixed[j, pl.ds(pl.multiple_of(block * T, T), T), :], wbuf[col, j],
                preferred_element_type=jnp.float32,
            )
        return total

    def give(col):
        return remote(psend.at[col], precv.at[col], pa_s.at[col], pa_r.at[col], partner)

    def give_part(col):
        psend[col] = part(1 - y, col).astype(jnp.bfloat16)
        give(col).start()

    def twin_part(n):
        for k in range(R):
            w_twin_in(k, n).wait_recv()
        give_part(lax.rem(g + G - n, G) * PAIR + 1 - c)

    give_part(f)
    twin_part(0)
    for n in range(1, G):
        w_across_in(R - 1, n).wait_recv()
        w_twin(R - 1, n).start()
    lax.fori_loop(0, R, attend_own, 0)
    for n in range(1, G):
        give_part(lax.rem(g + G - n, G) * PAIR + c)
    for n in range(1, G):
        twin_part(n)

    def keep_part(col, carry):
        acc[col] = part(y, col)
        return carry

    lax.fori_loop(0, F, keep_part, 0)

    staged[2].wait()
    staged[3].wait()
    total = jnp.zeros((T, 1), jnp.float32)
    for col in range(F):
        give(col).wait_recv()
        branch = (acc[col] + precv[col].astype(jnp.float32)) * (1.0 / math.sqrt(Dm))
        summed = resid_ref[:, col * C : (col + 1) * C].astype(jnp.float32) + branch
        acc[col] = summed
        total = total + jnp.sum(summed, axis=1, keepdims=True)
    mean = total / Dm
    square = jnp.zeros((T, 1), jnp.float32)
    for col in range(F):
        centered = acc[col] - mean
        square = square + jnp.sum(centered * centered, axis=1, keepdims=True)
    gain = lax.rsqrt(square / Dm + norm_epsilon)
    for col in range(F):
        at = slice(col * C, (col + 1) * C)
        out_ref[:, at] = (earlier_ref[:, at] + (acc[col] - mean) * gain) * (1.0 / TOP_K)

    def drain(j, carry):
        for comp in range(3):
            exchange(comp, j).wait_send()
        for d in range(2):
            for i in range(H):

                @pl.when(sends[d])
                def _():
                    halo(d, i, j).wait_send()

        @pl.when(j > 0)
        def _():
            w_line(j).wait_send()

        for n in range(1, G):
            w_across(j, n).wait_send()
        for n in range(G):
            w_twin(j, n).wait_send()
        return carry

    lax.fori_loop(0, R, drain, 0)

    def drain_parts(col, carry):
        give(col).wait_send()
        return carry

    lax.fori_loop(0, F, drain_parts, 0)


def segment_ids(utt_lengths, frames):
    order = jnp.arange(utt_lengths.shape[0])
    utt_ends = jnp.sum(jnp.where(order[None, :] <= order[:, None], utt_lengths[None, :], 0), axis=1)
    places = jnp.arange(frames, dtype=jnp.int32)
    return jnp.sum((places[:, None] >= utt_ends[None, :]).astype(jnp.int32), axis=1)


def attend_window(stacked, segment):
    frames = stacked.shape[0]
    longest = frames // 8
    rows_block = min(512, frames)
    key_span = min(frames, rows_block + 2 * longest)
    inverse_root = 1.0 / math.sqrt(stacked.shape[-1])
    queries = stacked[:, 0]
    keys_all = stacked[:, 1]
    values_all = stacked[:, 2]

    def one_block(row_start):
        key_start = jnp.clip(row_start - longest, 0, frames - key_span)
        block_queries = lax.dynamic_slice_in_dim(queries, row_start, rows_block, 0)
        query_segment = lax.dynamic_slice_in_dim(segment, row_start, rows_block, 0)
        block_keys = lax.dynamic_slice_in_dim(keys_all, key_start, key_span, 0)
        block_values = lax.dynamic_slice_in_dim(values_all, key_start, key_span, 0)
        key_segment = lax.dynamic_slice_in_dim(segment, key_start, key_span, 0)
        scores = (
            jnp.einsum(
                "qhd,khd->hqk", block_queries, block_keys, preferred_element_type=jnp.float32
            )
            * inverse_root
        )
        allowed = (query_segment[:, None] == key_segment[None, :])[None]
        scores = jnp.where(allowed, scores, masked_score)
        row_max = jnp.max(scores, axis=2, keepdims=True)
        weights = jnp.exp(scores - row_max)
        row_total = jnp.sum(weights, axis=2)
        summed = jnp.einsum(
            "hqk,khd->qhd",
            weights.astype(jnp.bfloat16),
            block_values,
            preferred_element_type=jnp.float32,
        )
        return (summed / jnp.transpose(row_total)[:, :, None]).astype(jnp.bfloat16)

    starts = jnp.arange(frames // rows_block, dtype=jnp.int32) * rows_block
    outputs = lax.map(one_block, starts)
    return outputs.reshape(frames, stacked.shape[2], stacked.shape[3])


def spread(qkv, resid, earlier, lengths, teacher_out, student_out):
    teacher_new = (
        ema_decay * teacher_out.astype(jnp.float32)
        + (1.0 - ema_decay) * student_out.astype(jnp.float32)
    ).astype(jnp.bfloat16)
    tokens = qkv.shape[1]
    groups = lax.axis_size("seq")
    frames = tokens * groups
    segment = segment_ids(lengths[0], frames)
    own_heads = qkv[0].reshape(tokens, 3, groups, HEADS // groups, HEAD_DIM)
    attended = attend_window(
        lax.all_to_all(own_heads, "seq", split_axis=2, concat_axis=0, tiled=True)[:, :, 0], segment
    )
    regathered = lax.all_to_all(attended[:, None], "seq", split_axis=0, concat_axis=1, tiled=True)
    mixed_rows = regathered.reshape(tokens, HEADS * HEAD_DIM)
    full_rows = lax.all_gather(teacher_new, "seq", axis=0, tiled=True)
    branch = jnp.dot(
        mixed_rows,
        lax.all_gather(full_rows, "fsdp", axis=1, tiled=True),
        preferred_element_type=jnp.float32,
    )
    branch = branch / math.sqrt(HEADS * HEAD_DIM)
    summed = resid[0].astype(jnp.float32) + branch
    centered = summed - jnp.mean(summed, axis=1, keepdims=True)
    normed = centered * lax.rsqrt(
        jnp.mean(centered * centered, axis=1, keepdims=True) + norm_epsilon
    )
    targets = ((earlier[0] + normed) / TOP_K)[None]
    return (targets, teacher_new)


def shards(F, S, qkv, resid, earlier, lengths, teacher_out, student_out):
    T, width = qkv.shape[1:]
    Dm = resid.shape[2]
    longest = T * S // 8
    H = -(-(longest - 1) // T)
    R, G, C, cw = S // PAIR, F // PAIR, Dm // F, Dm // S
    if S % PAIR or F % PAIR or H > PAIR or cw % 128 or C % 128 or T % 16:
        return spread(qkv, resid, earlier, lengths, teacher_out, student_out)
    nk = (2 * H + 1) * T
    vmem = pl.BlockSpec(memory_space=pltpu.VMEM)
    hbm = pl.BlockSpec(memory_space=pltpu.HBM)
    dma = pltpu.SemaphoreType.DMA
    targets, teacher_new = pl.pallas_call(
        functools.partial(body, F, S, H),
        out_shape=(
            jax.ShapeDtypeStruct((T, Dm), jnp.float32),
            jax.ShapeDtypeStruct(teacher_out.shape, jnp.bfloat16),
        ),
        in_specs=[pl.BlockSpec(memory_space=pltpu.SMEM)] + [hbm] * 5,
        out_specs=(vmem, vmem),
        scratch_shapes=[
            pltpu.VMEM((T, Dm), resid.dtype),
            pltpu.VMEM((T, Dm), earlier.dtype),
            pltpu.VMEM(teacher_out.shape, teacher_out.dtype),
            pltpu.VMEM(student_out.shape, student_out.dtype),
            dma((4,)),
            pltpu.VMEM((R, PAIR * T, cw), jnp.bfloat16),
            pltpu.VMEM((R, 2, (PAIR + 2 * H) * T, cw), jnp.bfloat16),
            pltpu.VMEM((R, PAIR * T, cw), jnp.bfloat16),
            pltpu.VMEM((F, R) + teacher_out.shape, jnp.bfloat16),
            pltpu.VMEM((PAIR, T, nk), jnp.float32),
            pltpu.VMEM((F, T, C), jnp.bfloat16),
            pltpu.VMEM((F, T, C), jnp.bfloat16),
            pltpu.VMEM((F, T, C), jnp.float32),
            dma((3, R)), dma((3, R)), dma((3, R)),
            dma((2, H, R)), dma((2, H, R)),
            dma((R,)), dma((R,)),
            dma((R, G)), dma((R, G)),
            dma((R, G)), dma((R, G)),
            dma((F,)), dma((F,)),
        ],
        compiler_params=pltpu.CompilerParams(
            collective_id=0, has_side_effects=True, vmem_limit_bytes=63 * 2**20
        ),
        cost_estimate=pl.CostEstimate(
            flops=4 * T * nk * Dm + 2 * T * Dm * Dm, bytes_accessed=2 * T * width + 14 * T * Dm,
            transcendentals=HEADS * T * nk,
        ),
    )(lengths, qkv[0], resid[0], earlier[0], teacher_out, student_out)
    return (targets[None], teacher_new)


def solution(mesh):
    placed = (
        P("fsdp", "seq", None),
        P("fsdp", "seq", None),
        P("fsdp", "seq", None),
        P("fsdp", None),
        P("seq", "fsdp"),
        P("seq", "fsdp"),
    )
    return jax.shard_map(
        functools.partial(shards, mesh.shape["fsdp"], mesh.shape["seq"]),
        mesh=mesh,
        in_specs=placed,
        out_specs=(P("fsdp", "seq", None), P("seq", "fsdp")),
        check_vma=False,
    )
```

```python
import functools
import math

import jax
import jax.numpy as jnp
from jax import lax
from jax.experimental import pallas as pl
from jax.experimental.pallas import tpu as pltpu
from jax.sharding import PartitionSpec as P

HEADS = 32
HEAD_DIM = 64
TOP_K = 8
PAIR = 2

ema_decay = 0.9
norm_epsilon = 1e-05
masked_score = -1e30
log2_e = math.log2(math.e)


def body(
    F, S, H,
    len_ref, qkv_ref, resid_hbm, earlier_hbm, tea_hbm, stu_hbm,
    out_ref, new_ref,
    resid_ref, earlier_ref, tea_ref, stu_ref, in_sem,
    q_buf, kv_buf, mixed, wbuf, bias, psend, precv, acc,
    yx_s, yx_r, loc, ha_s, ha_r, wz_s, wz_r, wx_s, wx_r, wc_s, wc_r, pa_s, pa_r,
):
    T = qkv_ref.shape[0]
    Dm = resid_hbm.shape[1]
    cw = Dm // S
    hd = Dm // HEADS
    hp = cw // hd
    R = S // PAIR
    G = F // PAIR
    C = Dm // F
    nk = (2 * H + 1) * T
    f = lax.axis_index("fsdp")
    s = lax.axis_index("seq")
    z, y = lax.div(s, PAIR), lax.rem(s, PAIR)
    g, c = lax.div(f, PAIR), lax.rem(f, PAIR)
    partner = (f, z * PAIR + 1 - y)
    twin = (g * PAIR + 1 - c, s)

    def line(k):
        return (f, lax.rem(z + k, R) * PAIR + y)

    def across(k):
        return (lax.rem(g + k, G) * PAIR + c, s)

    def cols(comp, j, half):
        return pl.ds(pl.multiple_of(comp * Dm + (PAIR * j + half) * cw, cw), cw)

    def place(comp, j, block):
        if comp == 0:
            return q_buf.at[j, pl.ds(pl.multiple_of(block * T, T), T), :]
        return kv_buf.at[j, comp - 1, pl.ds(pl.multiple_of((H + block) * T, T), T), :]

    def local(comp, j):
        return pltpu.make_async_copy(
            qkv_ref.at[:, cols(comp, j, y)], place(comp, j, y), loc.at[comp, j]
        )

    staged = [
        pltpu.make_async_copy(src, dst, in_sem.at[n])
        for n, (src, dst) in enumerate(
            ((tea_hbm, tea_ref), (stu_hbm, stu_ref), (resid_hbm, resid_ref), (earlier_hbm, earlier_ref))
        )
    ]
    for j in range(R):
        local(1, j).start()
        local(2, j).start()
    staged[0].start()
    staged[1].start()
    for j in range(R):
        local(0, j).start()

    barrier = pltpu.get_barrier_semaphore()
    peers = [partner, twin] + [line(k) for k in range(1, R)] + [across(k) for k in range(1, G)]
    for peer in peers:
        pl.semaphore_signal(barrier, inc=1, device_id=peer, device_id_type=pl.DeviceIdType.MESH)
    pl.semaphore_wait(barrier, len(peers))

    def remote(src, dst, send, recv, to):
        return pltpu.make_async_remote_copy(
            src_ref=src, dst_ref=dst, send_sem=send, recv_sem=recv,
            device_id=to, device_id_type=pl.DeviceIdType.MESH,
        )

    def exchange(comp, j):
        return remote(
            qkv_ref.at[:, cols(comp, j, 1 - y)], place(comp, j, y),
            yx_s.at[comp, j], yx_r.at[comp, j], partner,
        )

    def arrived(comp, j):
        return remote(
            qkv_ref.at[:, cols(comp, j, 1 - y)], place(comp, j, 1 - y),
            yx_s.at[comp, j], yx_r.at[comp, j], partner,
        )

    def halo(d, i, j):
        b, slot = (2 - H + i, i) if d == 0 else (i, H + 2 + i)
        to = (f, s + PAIR if d == 0 else s - PAIR)
        return remote(
            kv_buf.at[j, :, (H + b) * T : (H + b + 1) * T, :],
            kv_buf.at[j, :, slot * T : (slot + 1) * T, :],
            ha_s.at[d, i, j], ha_r.at[d, i, j], to,
        )

    sends = (z < R - 1, z > 0)
    comes = (z > 0, z < R - 1)

    def start_halos(j, own):
        for d in range(2):
            for i in range(H):
                b = 2 - H + i if d == 0 else i
                mine = (y == b) if own else (y != b)

                @pl.when(jnp.logical_and(mine, sends[d]))
                def _():
                    halo(d, i, j).start()

    def w_block(d, dist):
        return z - dist if d == 0 else z + dist

    def w_has(d, dist):
        return z >= dist if d == 0 else z + dist < R

    def w_pass(d, dist):
        at = wbuf.at[f, w_block(d, dist)]
        to = (f, s + PAIR if d == 0 else s - PAIR)
        return remote(at, at, wz_s.at[d, dist], wz_r.at[d, dist], to)

    def w_pass_in(d, dist):
        at = wbuf.at[f, w_block(d, dist)]
        to = (f, s + PAIR if d == 0 else s - PAIR)
        return remote(at, at, wz_s.at[d, dist - 1], wz_r.at[d, dist - 1], to)

    def w_spread(block):
        for n in range(1, G):
            w_across(block, n).start()
        w_twin(block, 0).start()

    def w_arrivals(dist):
        for d in range(2):

            @pl.when(w_has(d, dist))
            def _():
                w_pass_in(d, dist).wait_recv()

                @pl.when(sends[d])
                def _():
                    w_pass(d, dist).start()

                w_spread(w_block(d, dist))

    def w_share(block):
        for n in range(1, G):
            w_across_in(block, n).wait_recv()
            w_twin(block, n).start()

    def w_shares(dist):
        for d in range(2):

            @pl.when(w_has(d, dist))
            def _():
                w_share(w_block(d, dist))

    def w_across(k, n):
        at = wbuf.at[f, k]
        return remote(at, at, wx_s.at[k, n], wx_r.at[k, n], across(n))

    def w_across_in(k, n):
        at = wbuf.at[lax.rem(g + G - n, G) * PAIR + c, k]
        return remote(at, at, wx_s.at[k, n], wx_r.at[k, n], across(n))

    def w_twin(k, n):
        at = wbuf.at[lax.rem(g + G - n, G) * PAIR + c, k]
        return remote(at, at, wc_s.at[k, n], wc_r.at[k, n], twin)

    def w_twin_in(k, n):
        at = wbuf.at[lax.rem(g + G - n, G) * PAIR + 1 - c, k]
        return remote(at, at, wc_s.at[k, n], wc_r.at[k, n], twin)

    for j in range(R):
        exchange(1, j).start()
        exchange(2, j).start()
        if j > 0:
            exchange(0, j - 1).start()
    exchange(0, R - 1).start()

    for j in range(R):
        local(1, j).wait()
        local(2, j).wait()
        start_halos(j, True)

    staged[0].wait()
    staged[1].wait()
    new = (
        ema_decay * tea_ref[...].astype(jnp.float32)
        + (1.0 - ema_decay) * stu_ref[...].astype(jnp.float32)
    ).astype(jnp.bfloat16)
    new_ref[...] = new
    wbuf[f, z] = new
    for d in range(2):

        @pl.when(sends[d])
        def _():
            w_pass(d, 0).start()

    w_spread(z)
    staged[2].start()
    staged[3].start()

    @pl.when(z == 0)
    def _():
        kv_buf[:, :, 0 : H * T, :] = jnp.zeros((R, 2, H * T, cw), jnp.bfloat16)

    @pl.when(z == R - 1)
    def _():
        kv_buf[:, :, (H + 2) * T :, :] = jnp.zeros((R, 2, H * T, cw), jnp.bfloat16)

    for b in range(2):
        first = z * (PAIR * T) + b * T
        rows = first + lax.broadcasted_iota(jnp.int32, (T, nk), 0)
        keys = first - H * T + lax.broadcasted_iota(jnp.int32, (T, nk), 1)
        row_segment = jnp.zeros((T, nk), jnp.int32)
        key_segment = jnp.where(jnp.logical_or(keys < 0, keys >= S * T), -1, 0)
        end = 0
        for n in range(len_ref.shape[1]):
            end = end + len_ref[0, n]
            row_segment = row_segment + (rows >= end).astype(jnp.int32)
            key_segment = key_segment + (keys >= end).astype(jnp.int32)
        outside = jnp.logical_or(keys < 0, keys >= S * T)
        same = jnp.logical_and(row_segment == key_segment, jnp.logical_not(outside))
        bias[b] = jnp.where(same, 0.0, masked_score)

    def forward(j):
        arrived(1, j).wait_recv()
        arrived(2, j).wait_recv()
        start_halos(j, False)

    forward(0)

    scale = log2_e / math.sqrt(hd)

    def attend(j, carry):
        @pl.when(j < R - 1)
        def _():
            forward(j + 1)
            w_arrivals(j + 1)

        @pl.when(j == 1)
        def _():
            w_share(z)

        @pl.when(j > 1)
        def _():
            w_shares(j - 1)

        local(0, j).wait()
        arrived(0, j).wait_recv()
        for d in range(2):
            for i in range(H):

                @pl.when(comes[d])
                def _():
                    halo(d, i, j).wait_recv()

        head_of = lax.broadcasted_iota(jnp.int32, (T, cw), 1) // hd
        for b in range(2):
            query = q_buf[j, b * T : (b + 1) * T, :].astype(jnp.float32)
            key = kv_buf[j, 0, b * T : b * T + nk, :]
            value = kv_buf[j, 1, b * T : b * T + nk, :]
            stacked = jnp.concatenate(
                [jnp.where(head_of == h, query, 0.0).astype(jnp.bfloat16) for h in range(hp)], axis=0
            )
            scores = lax.dot_general(
                stacked, key, (((1,), (1,)), ((), ())), preferred_element_type=jnp.float32
            )
            scores = scores.reshape(hp, T, nk) * scale + bias[b][None]
            weights = jnp.exp2(scores - jnp.max(scores, axis=2, keepdims=True))
            total = jnp.sum(weights, axis=2, keepdims=True)
            summed = jnp.dot(
                weights.astype(jnp.bfloat16).reshape(hp * T, nk), value,
                preferred_element_type=jnp.float32,
            ).reshape(hp, T, cw) / total
            picked = summed[0]
            for h in range(1, hp):
                picked = jnp.where(head_of == h, summed[h], picked)
            mixed[j, b * T : (b + 1) * T, :] = picked.astype(jnp.bfloat16)
        return carry

    lax.fori_loop(0, R, attend, 0)

    def part(block, col):
        total = jnp.zeros((T, C), jnp.float32)
        for j in range(R):
            total = total + jnp.dot(
                mixed[j, pl.ds(pl.multiple_of(block * T, T), T), :], wbuf[col, j],
                preferred_element_type=jnp.float32,
            )
        return total

    def give(col):
        return remote(psend.at[col], precv.at[col], pa_s.at[col], pa_r.at[col], partner)

    def give_part(col):
        psend[col] = part(1 - y, col).astype(jnp.bfloat16)
        give(col).start()

    def twin_part(n):
        for k in range(R):
            w_twin_in(k, n).wait_recv()
        give_part(lax.rem(g + G - n, G) * PAIR + 1 - c)

    give_part(f)
    twin_part(0)
    if R > 1:
        w_shares(R - 1)
    else:
        w_share(z)
    for n in range(1, G):
        give_part(lax.rem(g + G - n, G) * PAIR + c)
    for n in range(1, G):
        twin_part(n)

    def keep_part(col, carry):
        acc[col] = part(y, col)
        return carry

    lax.fori_loop(0, F, keep_part, 0)

    staged[2].wait()
    staged[3].wait()
    total = jnp.zeros((T, 1), jnp.float32)
    for col in range(F):
        give(col).wait_recv()
        branch = (acc[col] + precv[col].astype(jnp.float32)) * (1.0 / math.sqrt(Dm))
        summed = resid_ref[:, col * C : (col + 1) * C].astype(jnp.float32) + branch
        acc[col] = summed
        total = total + jnp.sum(summed, axis=1, keepdims=True)
    mean = total / Dm
    square = jnp.zeros((T, 1), jnp.float32)
    for col in range(F):
        centered = acc[col] - mean
        square = square + jnp.sum(centered * centered, axis=1, keepdims=True)
    gain = lax.rsqrt(square / Dm + norm_epsilon)
    for col in range(F):
        at = slice(col * C, (col + 1) * C)
        out_ref[:, at] = (earlier_ref[:, at] + (acc[col] - mean) * gain) * (1.0 / TOP_K)

    def drain(j, carry):
        for comp in range(3):
            exchange(comp, j).wait_send()
        for d in range(2):
            for i in range(H):

                @pl.when(sends[d])
                def _():
                    halo(d, i, j).wait_send()

        for d in range(2):

            @pl.when(jnp.logical_and(w_has(d, j), sends[d]))
            def _():
                w_pass(d, j).wait_send()

        for n in range(1, G):
            w_across(j, n).wait_send()
        for n in range(G):
            w_twin(j, n).wait_send()
        return carry

    lax.fori_loop(0, R, drain, 0)

    def drain_parts(col, carry):
        give(col).wait_send()
        return carry

    lax.fori_loop(0, F, drain_parts, 0)


def segment_ids(utt_lengths, frames):
    order = jnp.arange(utt_lengths.shape[0])
    utt_ends = jnp.sum(jnp.where(order[None, :] <= order[:, None], utt_lengths[None, :], 0), axis=1)
    places = jnp.arange(frames, dtype=jnp.int32)
    return jnp.sum((places[:, None] >= utt_ends[None, :]).astype(jnp.int32), axis=1)


def attend_window(stacked, segment):
    frames = stacked.shape[0]
    longest = frames // 8
    rows_block = min(512, frames)
    key_span = min(frames, rows_block + 2 * longest)
    inverse_root = 1.0 / math.sqrt(stacked.shape[-1])
    queries = stacked[:, 0]
    keys_all = stacked[:, 1]
    values_all = stacked[:, 2]

    def one_block(row_start):
        key_start = jnp.clip(row_start - longest, 0, frames - key_span)
        block_queries = lax.dynamic_slice_in_dim(queries, row_start, rows_block, 0)
        query_segment = lax.dynamic_slice_in_dim(segment, row_start, rows_block, 0)
        block_keys = lax.dynamic_slice_in_dim(keys_all, key_start, key_span, 0)
        block_values = lax.dynamic_slice_in_dim(values_all, key_start, key_span, 0)
        key_segment = lax.dynamic_slice_in_dim(segment, key_start, key_span, 0)
        scores = (
            jnp.einsum(
                "qhd,khd->hqk", block_queries, block_keys, preferred_element_type=jnp.float32
            )
            * inverse_root
        )
        allowed = (query_segment[:, None] == key_segment[None, :])[None]
        scores = jnp.where(allowed, scores, masked_score)
        row_max = jnp.max(scores, axis=2, keepdims=True)
        weights = jnp.exp(scores - row_max)
        row_total = jnp.sum(weights, axis=2)
        summed = jnp.einsum(
            "hqk,khd->qhd",
            weights.astype(jnp.bfloat16),
            block_values,
            preferred_element_type=jnp.float32,
        )
        return (summed / jnp.transpose(row_total)[:, :, None]).astype(jnp.bfloat16)

    starts = jnp.arange(frames // rows_block, dtype=jnp.int32) * rows_block
    outputs = lax.map(one_block, starts)
    return outputs.reshape(frames, stacked.shape[2], stacked.shape[3])


def spread(qkv, resid, earlier, lengths, teacher_out, student_out):
    teacher_new = (
        ema_decay * teacher_out.astype(jnp.float32)
        + (1.0 - ema_decay) * student_out.astype(jnp.float32)
    ).astype(jnp.bfloat16)
    tokens = qkv.shape[1]
    groups = lax.axis_size("seq")
    frames = tokens * groups
    segment = segment_ids(lengths[0], frames)
    own_heads = qkv[0].reshape(tokens, 3, groups, HEADS // groups, HEAD_DIM)
    attended = attend_window(
        lax.all_to_all(own_heads, "seq", split_axis=2, concat_axis=0, tiled=True)[:, :, 0], segment
    )
    regathered = lax.all_to_all(attended[:, None], "seq", split_axis=0, concat_axis=1, tiled=True)
    mixed_rows = regathered.reshape(tokens, HEADS * HEAD_DIM)
    full_rows = lax.all_gather(teacher_new, "seq", axis=0, tiled=True)
    branch = jnp.dot(
        mixed_rows,
        lax.all_gather(full_rows, "fsdp", axis=1, tiled=True),
        preferred_element_type=jnp.float32,
    )
    branch = branch / math.sqrt(HEADS * HEAD_DIM)
    summed = resid[0].astype(jnp.float32) + branch
    centered = summed - jnp.mean(summed, axis=1, keepdims=True)
    normed = centered * lax.rsqrt(
        jnp.mean(centered * centered, axis=1, keepdims=True) + norm_epsilon
    )
    targets = ((earlier[0] + normed) / TOP_K)[None]
    return (targets, teacher_new)


def shards(F, S, qkv, resid, earlier, lengths, teacher_out, student_out):
    T, width = qkv.shape[1:]
    Dm = resid.shape[2]
    longest = T * S // 8
    H = -(-(longest - 1) // T)
    R, G, C, cw = S // PAIR, F // PAIR, Dm // F, Dm // S
    if S % PAIR or F % PAIR or H > PAIR or cw % 128 or C % 128 or T % 16:
        return spread(qkv, resid, earlier, lengths, teacher_out, student_out)
    nk = (2 * H + 1) * T
    vmem = pl.BlockSpec(memory_space=pltpu.VMEM)
    hbm = pl.BlockSpec(memory_space=pltpu.HBM)
    dma = pltpu.SemaphoreType.DMA
    targets, teacher_new = pl.pallas_call(
        functools.partial(body, F, S, H),
        out_shape=(
            jax.ShapeDtypeStruct((T, Dm), jnp.float32),
            jax.ShapeDtypeStruct(teacher_out.shape, jnp.bfloat16),
        ),
        in_specs=[pl.BlockSpec(memory_space=pltpu.SMEM)] + [hbm] * 5,
        out_specs=(vmem, vmem),
        scratch_shapes=[
            pltpu.VMEM((T, Dm), resid.dtype),
            pltpu.VMEM((T, Dm), earlier.dtype),
            pltpu.VMEM(teacher_out.shape, teacher_out.dtype),
            pltpu.VMEM(student_out.shape, student_out.dtype),
            dma((4,)),
            pltpu.VMEM((R, PAIR * T, cw), jnp.bfloat16),
            pltpu.VMEM((R, 2, (PAIR + 2 * H) * T, cw), jnp.bfloat16),
            pltpu.VMEM((R, PAIR * T, cw), jnp.bfloat16),
            pltpu.VMEM((F, R) + teacher_out.shape, jnp.bfloat16),
            pltpu.VMEM((PAIR, T, nk), jnp.float32),
            pltpu.VMEM((F, T, C), jnp.bfloat16),
            pltpu.VMEM((F, T, C), jnp.bfloat16),
            pltpu.VMEM((F, T, C), jnp.float32),
            dma((3, R)), dma((3, R)), dma((3, R)),
            dma((2, H, R)), dma((2, H, R)),
            dma((2, R)), dma((2, R)),
            dma((R, G)), dma((R, G)),
            dma((R, G)), dma((R, G)),
            dma((F,)), dma((F,)),
        ],
        compiler_params=pltpu.CompilerParams(
            collective_id=0, has_side_effects=True, vmem_limit_bytes=63 * 2**20
        ),
        cost_estimate=pl.CostEstimate(
            flops=4 * T * nk * Dm + 2 * T * Dm * Dm, bytes_accessed=2 * T * width + 14 * T * Dm,
            transcendentals=HEADS * T * nk,
        ),
    )(lengths, qkv[0], resid[0], earlier[0], teacher_out, student_out)
    return (targets[None], teacher_new)


def solution(mesh):
    placed = (
        P("fsdp", "seq", None),
        P("fsdp", "seq", None),
        P("fsdp", "seq", None),
        P("fsdp", None),
        P("seq", "fsdp"),
        P("seq", "fsdp"),
    )
    return jax.shard_map(
        functools.partial(shards, mesh.shape["fsdp"], mesh.shape["seq"]),
        mesh=mesh,
        in_specs=placed,
        out_specs=(P("fsdp", "seq", None), P("seq", "fsdp")),
        check_vma=False,
    )
```
